32 devices in a mesh: gx: 4 (over x, core), gy: 8 (over z, y).
Axes of the slice: x: 2, y: 2, z: 4, core: 2. Of those that a mesh axis runs over, the one named last changes fastest.
Arguments:
- blocks: float32 [4096, 4, 4096], P(('gx', 'gy')), may hold values from -0.75 to 0.75
- prolong: float32 [4096, 4096], P(('gx', 'gy')), may hold values from -2 to 2
- columns: int32 [4096, 4], P(('gx', 'gy')), may hold values from 0 to 4095, as said below
- aggregate: int32 [4096], P(('gx', 'gy')), may hold values from 0 to 2047, as said below
- column_slot: int32 [4096, 4], P(('gx', 'gy')), may hold values from 0 to 6, as said below
- owner_row: int32 [2048], P(('gx', 'gy')), may hold values from 0 to 2047, as said below
Outputs:
- merged_panel: float32 [4096, 7, 4096], P(('gx', 'gy'))
The draws below stay inside these ranges and needn't reach their ends.
Inputs may be any that keep to these rules, and one draw needn't show every extreme that they name: `columns`: row i lists i first, then 3 distinct other blocks within 3 of i. `aggregate`: fine rows 4p+2 to 4p+5 (mod 4096) form coarse rows 2p and 2p+1 in that order, the first taking 1 to 3 of them. column_slot[i, k] = (aggregate[columns[i, k]] - aggregate[i] + 3) mod 2048. `owner_row`: a permutation. Coarse row I is held by device I // 64 and stored on device owner_row[I] // 64, a device with the same gy index; every device stores exactly 64 rows, and at most 17 of the rows held by one device go to one device, a bound reached in every draw.
All inputs are finite; a program needn't handle non-finite values.
Results may differ from the reference program's by a relative error of at most 0.0003.
Values sent between devices are 32-bit elements; how exact they have to be, the bound alone decides.
No kernel may reach another device: no remote copies, remote signals or barrier semaphores. Data moves between devices by JAX's collectives and lax.ppermute only.
A program may use at most 192 MiB of HBM per device.

```python
import jax
import jax.numpy as jnp
from jax import lax

BS = 64
NNZ = 4
REACH = 3
SLOTS = 7
NB_DEV = 128
NCD = 64
FINE = 4096
COARSE = 2048
N_GX = 4
N_GY = 8


def aggregate_of(key):
    split_at = jax.random.randint(jax.random.fold_in(key, 11), (COARSE // 2,), 1, 4).astype(jnp.int32)
    block_index = jnp.arange(FINE, dtype=jnp.int32)
    shifted = jnp.remainder(block_index - 2, FINE)
    pair_index = shifted // 4
    position = shifted % 4
    return (2 * pair_index + (position >= split_at[pair_index]).astype(jnp.int32)).astype(jnp.int32)


def columns_of(key):
    block_index = jnp.arange(FINE, dtype=jnp.int32)
    offsets = jnp.concatenate([jnp.arange(-REACH, 0, dtype=jnp.int32), jnp.arange(1, REACH + 1, dtype=jnp.int32)])
    targets = block_index[:, None] + offsets[None, :]
    inside = (targets >= 0) & (targets < FINE)
    scores = jax.random.randint(jax.random.fold_in(key, 12), (FINE, 2 * REACH), 0, 4096).astype(jnp.int32)
    scores = scores * 8 + jnp.arange(2 * REACH, dtype=jnp.int32)[None, :]
    scores = jnp.where(inside, scores, -1)
    chosen = lax.top_k(scores, NNZ - 1)[1]
    picked = jnp.take_along_axis(targets, chosen, axis=1)
    return jnp.concatenate([block_index[:, None], picked], axis=1).astype(jnp.int32)


def draw_columns(key, part):
    return columns_of(key)


def draw_aggregate(key, part):
    return aggregate_of(key)


def draw_column_slot(key, part):
    groups = aggregate_of(key)
    linked = columns_of(key)
    return jnp.remainder(groups[linked] - groups[:, None] + REACH, COARSE).astype(jnp.int32)


def draw_owner_row(key, part):
    size_gx = N_GX
    size_gy = N_GY
    share = NCD // size_gx
    order_gx = jax.random.permutation(jax.random.fold_in(key, 13), size_gx)
    bumps = jnp.zeros((size_gx,), jnp.int32).at[order_gx[0]].add(1).at[order_gx[1]].add(-1)
    source = jnp.arange(size_gx, dtype=jnp.int32)
    counts = share + bumps[jnp.remainder(source[None, :] - source[:, None], size_gx)]
    running = jnp.cumsum(counts, axis=1)
    row_index = jnp.arange(NCD, dtype=jnp.int32)
    labels = jnp.sum((running[:, None, :] <= row_index[None, :, None]).astype(jnp.int32), axis=2)
    spread = jnp.broadcast_to(labels[:, None, :], (size_gx, size_gy, NCD))
    shuffled = jax.random.permutation(jax.random.fold_in(key, 14), spread, axis=2, independent=True)
    onehot = (shuffled[..., None] == source[None, None, None, :]).astype(jnp.int32)
    rank_in = jnp.sum((jnp.cumsum(onehot, axis=2) - onehot) * onehot, axis=3)
    earlier = jnp.cumsum(counts, axis=0) - counts
    source_grid = jnp.broadcast_to(source[:, None, None], (size_gx, size_gy, NCD))
    slot_index = earlier[source_grid, shuffled] + rank_in
    column_gy = jnp.arange(size_gy, dtype=jnp.int32)[None, :, None]
    stored = (shuffled * size_gy + column_gy) * NCD + slot_index
    return stored.reshape(-1).astype(jnp.int32)


def level_of(own_key, extent, pieces, least, largest):
    loudness, own = 1.0, jax.random.fold_in(own_key, 6)
    for dim, shards_of in pieces:
        heights = jnp.exp(jax.random.uniform(jax.random.fold_in(own, dim), (shards_of,), jnp.float32, least / len(pieces), largest / len(pieces)))
        loudness = loudness * jnp.repeat(heights, extent[dim] // shards_of).reshape([-1 if axis == dim else 1 for axis in range(len(extent))])
    return loudness


def normal_values(stream_key, dims, scale, limit, cuts=(), kind=jnp.bfloat16):
    loudness = level_of(stream_key, dims, cuts, -0.22, 0.18) if cuts else 1.0
    entries = jax.random.normal(stream_key, dims, jnp.float32) * scale * loudness
    return jnp.minimum(jnp.maximum(entries, -limit), limit).astype(kind)


def setup_inputs(seed: int = 0) -> dict:
    key_of = jax.random.split(jax.random.key(seed), 7)
    blocks = normal_values(key_of[0], (FINE, NNZ, BS * BS), BS ** -0.5, 0.75, ((0, 32),), jnp.float32)
    prolong = normal_values(key_of[1], (FINE, BS * BS), 0.35, 2.0, ((0, 32),), jnp.float32)
    columns = draw_columns(jax.random.fold_in(key_of[6], 71), 0)
    aggregate = draw_aggregate(jax.random.fold_in(key_of[6], 71), 0)
    column_slot = draw_column_slot(jax.random.fold_in(key_of[6], 71), 0)
    owner_row = draw_owner_row(jax.random.fold_in(key_of[6], 71), 0)
    return dict(blocks=blocks, prolong=prolong, columns=columns, aggregate=aggregate, column_slot=column_slot, owner_row=owner_row)


def galerkin_terms(block_rows, left_blocks, right_blocks):
    count = block_rows.shape[0]
    matrix = block_rows.reshape(count, NNZ, BS, BS)
    left_q = left_blocks.reshape(count, BS, BS)
    right_q = right_blocks.reshape(count, NNZ, BS, BS)
    product = jnp.einsum("ikab,ikbc->ikac", matrix, right_q, precision=lax.Precision.HIGHEST)
    sandwich = jnp.einsum("iba,ikbc->ikac", left_q, product, precision=lax.Precision.HIGHEST)
    return sandwich.reshape(count * NNZ, BS * BS)


def reference(blocks, prolong, columns, aggregate, column_slot, owner_row):
    slab_count = FINE // NB_DEV

    def add_slab(accumulated, slab_index):
        slab_start = (slab_index * NB_DEV).astype(jnp.int32)
        slab_blocks = lax.dynamic_slice_in_dim(blocks, slab_start, NB_DEV, 0)
        slab_columns = lax.dynamic_slice_in_dim(columns, slab_start, NB_DEV, 0)
        left_blocks = lax.dynamic_slice_in_dim(prolong, slab_start, NB_DEV, 0)
        slab_aggregate = lax.dynamic_slice_in_dim(aggregate, slab_start, NB_DEV, 0)
        slab_slots = lax.dynamic_slice_in_dim(column_slot, slab_start, NB_DEV, 0)
        right_blocks = prolong[slab_columns]
        values = galerkin_terms(slab_blocks, left_blocks, right_blocks)
        target = (slab_aggregate[:, None] * SLOTS + slab_slots).reshape(-1).astype(jnp.int32)
        return accumulated.at[target].add(values), None

    start_sum = jnp.zeros((COARSE * SLOTS, BS * BS), jnp.float32)
    accumulated, _ = lax.scan(add_slab, start_sum, jnp.arange(slab_count, dtype=jnp.int32))
    coarse = accumulated.reshape(COARSE, SLOTS, BS * BS)
    placed = jnp.zeros_like(coarse).at[owner_row].set(coarse)
    pair_count = COARSE // (2 * NCD)
    paired = placed.reshape(pair_count, 1, 2 * NCD, SLOTS, BS * BS)
    merged = jnp.broadcast_to(paired, (pair_count, 2, 2 * NCD, SLOTS, BS * BS))
    return merged.reshape(2 * COARSE, SLOTS, BS * BS)
```

```python
import functools

import jax
import jax.numpy as jnp
from jax import lax
from jax.experimental import pallas as pl
from jax.experimental.pallas import tpu as pltpu
from jax.sharding import PartitionSpec as P

BS = 64
NNZ = 4
SLOTS = 7
ROW_BLOCKS = 6
MOST_FINE = 3
LANES = 128
PACK = BS * BS // LANES
BEFORE = 1
LABEL_ROWS = 8
GROUP = 4
ROW_BITS = 10

F32 = jnp.float32
BF16 = jnp.bfloat16
ANY = pl.BlockSpec(memory_space=pl.ANY)
SMEM = pl.BlockSpec(memory_space=pltpu.SMEM)
VMEM = pl.BlockSpec(memory_space=pltpu.VMEM)


def half_lanes(shape):
    return lax.broadcasted_iota(jnp.int32, shape, 1) < LANES // 2


def turned(value):
    return pltpu.roll(value, LANES // 2, 1)


def split(value):
    high = value.astype(BF16)
    low = (value - high.astype(F32)).astype(BF16)
    return high, low


def prepare_kernel(fine_rows, q_ref, before_ref, after_ref, w_ref, t_ref, natural, flipped):
    left = half_lanes((PACK, LANES))
    left_tall = half_lanes((BS, LANES))

    def one(source, base, window, lane, fine):
        packed = source[pl.ds(base, PACK, stride=8), :]
        swapped = turned(packed)
        even = jnp.where(left, packed, swapped)
        odd = jnp.where(left, swapped, packed)
        natural[lane, pl.ds(0, PACK, stride=2), :] = even
        natural[lane, pl.ds(1, PACK, stride=2), :] = odd
        high, low = split(natural[lane])
        w_ref[window, 0:BS, :] = high
        w_ref[window, BS : 2 * BS, :] = low
        if fine is not None:
            stacked = jnp.concatenate([even, odd, even, odd], axis=0)
            flipped[lane] = stacked.T[0:BS]
            ordered = jnp.concatenate(
                [flipped[lane, pl.ds(0, PACK, stride=2), :], flipped[lane, pl.ds(1, PACK, stride=2), :]], axis=0
            )
            high, low = split(ordered)
            t_ref[fine] = jnp.where(left_tall, high.astype(F32), low.astype(F32)).astype(BF16)

    @pl.loop(0, fine_rows // 8)
    def _(group):
        for lane in range(8):
            row = group * 8 + lane
            one(q_ref, group * (8 * PACK) + lane, row + BEFORE, lane, row)

    one(before_ref, 7, 0, 0, None)
    for row in range(5):
        one(after_ref, row, fine_rows + BEFORE + row, row, fine_rows + row if row < 2 else None)


def bucket_kernel(
    shift,
    fine_rows,
    fine_total,
    home_count,
    rows_of_gx,
    capacity,
    most,
    me_ref,
    columns_ref,
    slots_ref,
    aggregate_ref,
    owner_ref,
    edge_ref,
    blocks_ref,
    edge_blocks_ref,
    w_ref,
    t_ref,
    token_ref,
    out_ref,
    stored,
    total,
    label_ref,
    fine_list,
    window_list,
    place_list,
    place_of,
    in_sem,
    out_sem,
):
    wanted = me_ref[0] ^ shift
    first_block = me_ref[1] * fine_rows
    flat = lax.broadcasted_iota(jnp.int32, (LABEL_ROWS, LANES), 0) * LANES + lax.broadcasted_iota(
        jnp.int32, (LABEL_ROWS, LANES), 1
    )

    def edge_or(ref, row, offset, k=None):
        own = row < fine_rows
        inside = jnp.where(own, row, 0)
        outside = jnp.where(own, 0, row - fine_rows)
        if k is None:
            return jnp.where(own, ref[inside], edge_ref[offset + outside])
        return jnp.where(own, ref[k, inside], edge_ref[offset + k * 2 + outside])

    def fetch(row, index):
        target = stored.at[pl.ds(pl.multiple_of(index * 2 * BS, 2 * BS), 2 * BS)]

        @pl.when(row < fine_rows)
        def _():
            pltpu.make_async_copy(blocks_ref.at[row], target, in_sem).start()

        @pl.when(row >= fine_rows)
        def _():
            pltpu.make_async_copy(edge_blocks_ref.at[row - fine_rows], target, in_sem).start()

    def coarse_row(local, carry):
        used, listed, labels = carry
        owner = owner_ref[local]
        match = owner // rows_of_gx == wanted
        start = (local // 2) * 4 + 2
        leading = edge_or(aggregate_ref, start, 4 * NNZ)
        size = (
            1
            + (edge_or(aggregate_ref, start + 1, 4 * NNZ) == leading).astype(jnp.int32)
            + (edge_or(aggregate_ref, start + 2, 4 * NNZ) == leading).astype(jnp.int32)
        )
        second = local % 2 == 1
        first_fine = jnp.where(second, start + size, start)
        count = jnp.where(second, 4 - size, size)
        for slot in range(SLOTS):
            place_of[slot] = -1

        def fine_row(step, inner):
            used, listed, labels = inner
            row = first_fine + step
            fetch(row, listed)
            fine_list[listed] = row
            for k in range(NNZ):
                slot = edge_or(slots_ref, row, 2 * NNZ, k)
                window = edge_or(columns_ref, row, 0, k) - first_block + BEFORE
                window = jnp.where(window < 0, window + fine_total, window)
                window = jnp.where(window >= fine_total, window - fine_total, window)
                seen = place_of[slot]
                new = seen < 0
                place = jnp.where(new, used, seen)
                place_of[slot] = place
                used = used + new.astype(jnp.int32)
                label = (slot * 2**ROW_BITS + owner % home_count).astype(F32)
                labels = jnp.where(flat == place, label, labels)
                window_list[listed * NNZ + k] = window
                place_list[listed * NNZ + k] = place
            return used, listed + 1, labels

        return lax.fori_loop(0, jnp.where(match, count, 0), fine_row, (used, listed, labels))

    used, listed, labels = lax.fori_loop(
        0, home_count, coarse_row, (jnp.int32(0), jnp.int32(0), jnp.zeros((LABEL_ROWS, LANES), F32))
    )
    label_ref[...] = jnp.where(flat == LABEL_ROWS * LANES - 1, used.astype(F32), labels)
    label_out = pltpu.make_async_copy(label_ref, out_ref.at[pl.ds(capacity * PACK, LABEL_ROWS)], out_sem.at[1])
    label_out.start()
    groups = (listed + GROUP - 1) // GROUP

    def filler(index, _):
        fine_list[index] = 0
        for k in range(NNZ):
            window_list[index * NNZ + k] = 0
            place_list[index * NNZ + k] = most
        return 0

    lax.fori_loop(listed, groups * GROUP, filler, 0)

    @pl.loop(0, most + 1)
    def _(place):
        total[pl.ds(pl.multiple_of(place * PACK, PACK), PACK), :] = jnp.zeros((PACK, LANES), F32)

    @pl.loop(0, listed)
    def _(index):
        pltpu.make_async_copy(blocks_ref.at[0], stored.at[pl.ds(0, 2 * BS)], in_sem).wait()

    left = half_lanes((PACK, LANES))
    left_tall = half_lanes((BS, LANES))

    @pl.loop(0, groups)
    def _(group):
        results = []
        for lane in range(GROUP):
            index = group * GROUP + lane
            products = []
            for k in range(NNZ):
                packed = stored[pl.ds(index * 2 * BS + k, PACK, stride=NNZ), :]
                high = packed.astype(BF16).astype(F32)
                low = packed - high
                even = jnp.where(left, high, turned(low))
                odd = jnp.where(left, turned(high), low)
                both = jnp.concatenate([even, odd], axis=0).astype(BF16)
                factor = w_ref[window_list[index * NNZ + k]]
                q_high = factor[0:BS]
                q_low = factor[BS : 2 * BS]
                products.append(
                    jnp.dot(
                        jnp.concatenate([both, both], axis=1),
                        jnp.concatenate([q_high, q_high, q_low, q_low], axis=0),
                        preferred_element_type=F32,
                    )
                )
            wide = jnp.concatenate(
                [
                    jnp.where(left_tall, products[0], products[1]),
                    jnp.where(left_tall, products[2], products[3]),
                ],
                axis=1,
            )
            high, low = split(wide)
            row = t_ref[fine_list[index]]
            results.append(
                jnp.dot(
                    jnp.concatenate([row, row], axis=1),
                    jnp.concatenate([high, high, low, low], axis=0),
                    preferred_element_type=F32,
                )
            )
        for lane in range(GROUP):
            index = group * GROUP + lane
            for pair in range(2):
                even = results[lane][0:PACK, pair * LANES : (pair + 1) * LANES]
                odd = results[lane][PACK:BS, pair * LANES : (pair + 1) * LANES]
                packed = [jnp.where(left, even, turned(odd)), jnp.where(left, turned(even), odd)]
                for k in range(2):
                    place = place_list[index * NNZ + pair * 2 + k]
                    where = pl.ds(pl.multiple_of(place * PACK, PACK), PACK)
                    total[where, :] = total[where, :] + packed[k]

    main_out = pltpu.make_async_copy(
        total.at[pl.ds(0, capacity * PACK)], out_ref.at[pl.ds(0, capacity * PACK)], out_sem.at[0]
    )
    main_out.start()
    main_out.wait()
    label_out.wait()


def place_kernel(counts, capacity, home_count, clear, me_ref, *refs):
    own_count, partner_count = counts
    sources = refs[: own_count + partner_count]
    rest = refs[own_count + partner_count :]
    out_ref, labels, zeros, label_sem, zero_sem, sem = rest[-6:]
    slots, row_groups = out_ref.shape[0], out_ref.shape[1]
    copies = []
    for which, source in enumerate(sources):
        copies.append(
            pltpu.make_async_copy(
                source.at[pl.ds(capacity * PACK, LABEL_ROWS)], labels.at[which], label_sem.at[which]
            )
        )
        copies[-1].start()
    if clear:
        zeros[...] = jnp.zeros_like(zeros)

        @pl.loop(0, slots)
        def _(slot):
            @pl.loop(0, row_groups)
            def _(group):
                pltpu.make_async_copy(zeros, out_ref.at[slot, group], zero_sem).start()

        @pl.loop(0, slots * row_groups)
        def _(step):
            pltpu.make_async_copy(zeros, out_ref.at[0, 0], zero_sem).wait()

    moved = jnp.int32(0)
    for which, source in enumerate(sources):
        copies[which].wait()
        upper = me_ref[2] if which < own_count else 1 - me_ref[2]
        used = labels[which, LABEL_ROWS - 1, 0, LANES - 1].astype(jnp.int32)

        @pl.loop(0, used)
        def _(place):
            label = labels[which, place // LANES, 0, place % LANES].astype(jnp.int32)
            slot = label // 2**ROW_BITS
            row = label % 2**ROW_BITS + upper * home_count
            pltpu.make_async_copy(
                source.at[pl.ds(place * PACK, PACK)], out_ref.at[slot, row // 8, :, row % 8], sem
            ).start()

        moved = moved + used

    @pl.loop(0, moved)
    def _(step):
        pltpu.make_async_copy(sources[0].at[pl.ds(0, PACK)], out_ref.at[0, 0, :, 0], sem).wait()


def placed_into(out, out_type, me, own, partner, capacity, home_count):
    sources = [value.reshape(-1, 1, LANES) for value in own + partner]
    clear = out is None
    return pl.pallas_call(
        functools.partial(place_kernel, (len(own), len(partner)), capacity, home_count, clear),
        in_specs=[SMEM] + [ANY] * (len(sources) + (0 if clear else 1)),
        out_specs=ANY,
        out_shape=out_type,
        input_output_aliases={} if clear else {len(sources) + 1: 0},
        scratch_shapes=[
            pltpu.SMEM((len(sources), LABEL_ROWS, 1, LANES), F32),
            pltpu.VMEM((PACK, 8, 1, LANES), F32),
            pltpu.SemaphoreType.DMA((len(sources),)),
            pltpu.SemaphoreType.DMA,
            pltpu.SemaphoreType.DMA,
        ],
        compiler_params=pltpu.CompilerParams(vmem_limit_bytes=32 * 2**20),
    )(me, *sources, *([] if clear else [out]))


def body(blocks, prolong, columns, aggregate, column_slot, owner_row):
    fine_rows = blocks.shape[0]
    home_count = owner_row.shape[0]
    size_gx = lax.axis_size("gx")
    size_gy = lax.axis_size("gy")
    size = size_gx * size_gy
    here_gx = lax.axis_index("gx")
    here_gy = lax.axis_index("gy")
    position = lax.axis_index(("gx", "gy"))
    most = (home_count // size_gx + 1) * ROW_BLOCKS
    capacity = most
    most_fine = -(-(home_count // size_gx + 1) * MOST_FINE // GROUP) * GROUP
    me = jnp.stack([here_gx, position, here_gy % 2]).astype(jnp.int32)

    block_view = (
        blocks.reshape(fine_rows, NNZ, PACK, LANES).transpose(0, 2, 1, 3).reshape(fine_rows, NNZ * PACK, LANES)
    )
    q_view = (
        prolong.reshape(fine_rows // 8, 8, PACK, LANES).transpose(0, 2, 1, 3).reshape(fine_rows * PACK, LANES)
    )
    group_rows = 8 * PACK
    backward = [(i, (i - 1) % size) for i in range(size)]
    forward = [(i, (i + 1) % size) for i in range(size)]
    axes = ("gx", "gy")
    edge_ints = jnp.concatenate(
        [columns.T[:, :2].reshape(-1), column_slot.T[:, :2].reshape(-1), aggregate[:2]]
    )
    edge_ints = lax.ppermute(edge_ints, axes, backward)
    after = lax.ppermute(q_view[:group_rows], axes, backward)
    edge_blocks = lax.ppermute(block_view[:2], axes, backward)
    before = lax.ppermute(q_view[-group_rows:], axes, forward)

    right, left = pl.pallas_call(
        functools.partial(prepare_kernel, fine_rows),
        in_specs=[VMEM] * 3,
        out_specs=[VMEM] * 2,
        out_shape=[
            jax.ShapeDtypeStruct((fine_rows + BEFORE + 5, 2 * BS, LANES), BF16),
            jax.ShapeDtypeStruct((fine_rows + 2, BS, LANES), BF16),
        ],
        scratch_shapes=[pltpu.VMEM((8, BS, LANES), F32), pltpu.VMEM((8, BS, LANES), F32)],
        compiler_params=pltpu.CompilerParams(vmem_limit_bytes=32 * 2**20),
    )(q_view, before, after)

    def bucket(shift, token):
        return pl.pallas_call(
            functools.partial(
                bucket_kernel,
                shift,
                fine_rows,
                fine_rows * size,
                home_count,
                home_count * size_gy,
                capacity,
                most,
            ),
            in_specs=[SMEM] * 6 + [ANY] * 2 + [VMEM] * 2 + [ANY],
            out_specs=ANY,
            out_shape=jax.ShapeDtypeStruct((capacity * PACK + LABEL_ROWS, LANES), F32),
            scratch_shapes=[
                pltpu.VMEM((most_fine * 2 * BS, LANES), F32),
                pltpu.VMEM(((most + 1) * PACK, LANES), F32),
                pltpu.VMEM((LABEL_ROWS, LANES), F32),
                pltpu.SMEM((most_fine,), jnp.int32),
                pltpu.SMEM((most_fine * NNZ,), jnp.int32),
                pltpu.SMEM((most_fine * NNZ,), jnp.int32),
                pltpu.SMEM((8,), jnp.int32),
                pltpu.SemaphoreType.DMA,
                pltpu.SemaphoreType.DMA((2,)),
            ],
            compiler_params=pltpu.CompilerParams(vmem_limit_bytes=40 * 2**20),
        )(
            me,
            columns.T,
            column_slot.T,
            aggregate,
            owner_row,
            edge_ints,
            block_view,
            edge_blocks,
            right,
            left,
            token,
        )

    def across(value, shift):
        pairs = [(source, source ^ shift) for source in range(size_gx)]
        return lax.ppermute(value, "gx", pairs)

    def partner(value):
        pairs = [(source, source ^ 1) for source in range(size_gy)]
        return lax.ppermute(value, "gy", pairs)

    own_sent = bucket(0, me)
    own_partner = partner(own_sent)
    arrived = []
    token = own_sent
    for shift in list(range(2, size_gx)) + [1]:
        sent = bucket(shift, token)
        token = sent
        arrived.append(across(sent, shift))
    arrived = arrived[-1:] + arrived[:-1]
    from_partner = [partner(value) for value in arrived]

    out_type = jax.ShapeDtypeStruct((SLOTS, 2 * home_count // 8, PACK, 8, 1, LANES), F32)
    common = (out_type, me)
    limits = (capacity, home_count)
    out = placed_into(None, *common, [own_sent] + arrived, [], *limits)
    out = placed_into(out, *common, [], [own_partner, from_partner[0]], *limits)
    for value in from_partner[1:]:
        out = placed_into(out, *common, [], [value], *limits)
    return (
        out.reshape(SLOTS, 2 * home_count // 8, PACK, 8, LANES)
        .transpose(1, 3, 0, 2, 4)
        .reshape(2 * home_count, SLOTS, BS * BS)
    )


def solution(mesh):
    placed = (
        P(("gx", "gy"), None, None),
        P(("gx", "gy"), None),
        P(("gx", "gy"), None),
        P(("gx", "gy")),
        P(("gx", "gy"), None),
        P(("gx", "gy")),
    )
    return jax.shard_map(
        body, mesh=mesh, in_specs=placed, out_specs=P(("gx", "gy"), None, None), check_vma=False
    )
```

```python
import functools

import jax
import jax.numpy as jnp
from jax import lax
from jax.experimental import pallas as pl
from jax.experimental.pallas import tpu as pltpu
from jax.sharding import PartitionSpec as P

BS = 64
NNZ = 4
SLOTS = 7
ROW_BLOCKS = 6
MOST_FINE = 3
LANES = 128
PACK = BS * BS // LANES
BEFORE = 1
AFTER = 5
LABEL_ROWS = 8
GROUP = 4
ROW_BITS = 10
FIRST_ROUND = 9

F32 = jnp.float32
BF16 = jnp.bfloat16
ANY = pl.BlockSpec(memory_space=pl.ANY)
HBM = pl.BlockSpec(memory_space=pltpu.HBM)
SMEM = pl.BlockSpec(memory_space=pltpu.SMEM)
VMEM = pl.BlockSpec(memory_space=pltpu.VMEM)


def cost_of(seconds):
    return pl.CostEstimate(flops=int(seconds * 1e15), bytes_accessed=int(seconds * 3e12), transcendentals=0)


SMALL = cost_of(1e-6)


def half_lanes(shape):
    return lax.broadcasted_iota(jnp.int32, shape, 1) < LANES // 2


def turned(value):
    return pltpu.roll(value, LANES // 2, 1)


def split(value):
    high = value.astype(BF16)
    low = (value - high.astype(F32)).astype(BF16)
    return high, low


def factors(packed, natural):
    left = half_lanes((PACK, LANES))
    swapped = turned(packed)
    even = jnp.where(left, packed, swapped)
    odd = jnp.where(left, swapped, packed)
    natural[pl.ds(0, PACK, stride=2), :] = even
    natural[pl.ds(1, PACK, stride=2), :] = odd
    high, low = split(natural[...])
    return even, odd, high, low


def transposed(even, odd, flipped):
    flipped[...] = jnp.concatenate([even, odd, even, odd], axis=0).T[0:BS]
    ordered = jnp.concatenate(
        [flipped[pl.ds(0, PACK, stride=2), :], flipped[pl.ds(1, PACK, stride=2), :]], axis=0
    )
    high, low = split(ordered)
    return jnp.where(half_lanes((BS, LANES)), high.astype(F32), low.astype(F32)).astype(BF16)


def prepare_kernel(fine_rows, q_ref, w_ref, t_ref, natural, flipped):
    @pl.loop(0, fine_rows // 8)
    def _(group):
        for lane in range(8):
            row = group * 8 + lane
            packed = q_ref[pl.ds(group * (8 * PACK) + lane, PACK, stride=8), :]
            even, odd, high, low = factors(packed, natural.at[lane])
            w_ref[row + BEFORE, 0:BS, :] = high
            w_ref[row + BEFORE, BS : 2 * BS, :] = low
            t_ref[row] = transposed(even, odd, flipped.at[lane])


def prepare_edge_kernel(
    fine_rows, before_ref, after_ref, w_in, t_in, w_ref, t_ref, w_edge, t_edge, natural, flipped, sem
):
    for row in range(AFTER + BEFORE):
        source, base = (before_ref, 7) if row == AFTER else (after_ref, row)
        even, odd, high, low = factors(source[pl.ds(base, PACK, stride=8), :], natural.at[row])
        w_edge[row, 0:BS, :] = high
        w_edge[row, BS : 2 * BS, :] = low
        if row < 2:
            t_edge[row] = transposed(even, odd, flipped.at[row])
    copies = [
        pltpu.make_async_copy(w_edge.at[pl.ds(0, AFTER)], w_ref.at[pl.ds(fine_rows + BEFORE, AFTER)], sem.at[0]),
        pltpu.make_async_copy(w_edge.at[pl.ds(AFTER, BEFORE)], w_ref.at[pl.ds(0, BEFORE)], sem.at[1]),
        pltpu.make_async_copy(t_edge, t_ref.at[pl.ds(fine_rows, 2)], sem.at[2]),
    ]
    for copy in copies:
        copy.start()
    for copy in copies:
        copy.wait()


def bucket_kernel(
    shift,
    base,
    capacity,
    fine_rows,
    fine_total,
    home_count,
    rows_of_gx,
    me_ref,
    columns_ref,
    slots_ref,
    aggregate_ref,
    owner_ref,
    edge_ref,
    blocks_ref,
    edge_blocks_ref,
    w_ref,
    t_ref,
    token_ref,
    out_ref,
    used_ref,
    stored,
    fine_list,
    table_list,
    local_list,
    place_of,
    in_sem,
):
    lowest = (me_ref[0] ^ shift) * rows_of_gx
    first_block = me_ref[1] * fine_rows
    flat = lax.broadcasted_iota(jnp.int32, (LABEL_ROWS, LANES), 0) * LANES + lax.broadcasted_iota(
        jnp.int32, (LABEL_ROWS, LANES), 1
    )

    def listing(pair, groups, carry):
        listed, tables, own = carry
        start = pair * 4 + 2
        size = 1 + (groups[1] == groups[0]).astype(jnp.int32) + (groups[2] == groups[0]).astype(jnp.int32)
        owners = [owner_ref[pair * 2], owner_ref[pair * 2 + 1]]
        match = [((owner >= lowest) & (owner < lowest + rows_of_gx)).astype(jnp.int32) for owner in owners]
        local = [lax.rem(owner, home_count) for owner in owners]
        table = [tables, tables + match[0]]
        for step in range(4):
            second = size <= step
            fine_list[listed] = start + step
            table_list[listed] = jnp.where(second, table[1], table[0]) * 8
            local_list[listed] = jnp.where(second, local[1], local[0])
            listed = listed + jnp.where(second, match[1], match[0])
            own = jnp.where(start + step < fine_rows, listed, own)
        return listed, tables + match[0] + match[1], own

    zero = jnp.int32(0)
    last = home_count // 2 - 1
    carry = lax.fori_loop(
        0,
        last,
        lambda pair, carry: listing(pair, [aggregate_ref[pair * 4 + 2 + step] for step in range(3)], carry),
        (zero, zero, zero),
    )
    edge_groups = [aggregate_ref[last * 4 + 2], aggregate_ref[last * 4 + 3], edge_ref[4 * NNZ]]
    listed, tables, own = listing(last, edge_groups, carry)

    def target(index):
        return stored.at[pl.ds(pl.multiple_of(index * 2 * BS, 2 * BS), 2 * BS)]

    @pl.loop(0, own)
    def _(index):
        pltpu.make_async_copy(blocks_ref.at[fine_list[index]], target(index), in_sem).start()

    @pl.loop(own, listed)
    def _(index):
        pltpu.make_async_copy(edge_blocks_ref.at[fine_list[index] - fine_rows], target(index), in_sem).start()

    @pl.loop(0, tables)
    def _(table):
        for slot in range(SLOTS):
            place_of[table * 8 + slot] = -1

    @pl.loop(0, capacity)
    def _(place):
        out_ref[pl.ds(pl.multiple_of(place * PACK, PACK), PACK), :] = jnp.zeros((PACK, LANES), F32)

    groups = (listed + GROUP - 1) // GROUP

    @pl.loop(listed, groups * GROUP)
    def _(index):
        fine_list[index] = 2
        table_list[index] = 0
        local_list[index] = 0

    @pl.loop(0, listed)
    def _(index):
        pltpu.make_async_copy(blocks_ref.at[0], target(0), in_sem).wait()

    left = half_lanes((PACK, LANES))
    left_tall = half_lanes((BS, LANES))

    def main(group, carry):
        used, labels = carry
        results = []
        places = []
        for lane in range(GROUP):
            index = group * GROUP + lane
            real = index < listed
            row = fine_list[index]
            inside = row < fine_rows
            own_row = jnp.where(inside, row, 0)
            edge_row = jnp.where(inside, 0, row - fine_rows)
            products = []
            for k in range(NNZ):
                column = jnp.where(inside, columns_ref[k, own_row], edge_ref[k * 2 + edge_row])
                window = column - first_block + BEFORE
                window = jnp.where(window < 0, window + fine_total, window)
                window = jnp.where(window >= fine_total, window - fine_total, window)
                slot = jnp.where(inside, slots_ref[k, own_row], edge_ref[2 * NNZ + k * 2 + edge_row])
                entry = table_list[index] + slot
                seen = place_of[entry]
                new = (seen < 0) & real
                place = jnp.where(new, used, seen)
                place_of[entry] = place
                used = used + new.astype(jnp.int32)
                valid = real & (place >= base) & (place < base + capacity)
                place = jnp.where(valid, place - base, 0)
                places.append((valid, place))
                label = (slot * 2**ROW_BITS + local_list[index]).astype(F32)
                labels = jnp.where((flat == place) & valid, label, labels)
                packed = stored[pl.ds(index * 2 * BS + k, PACK, stride=NNZ), :]
                high = packed.astype(BF16).astype(F32)
                low = packed - high
                even = jnp.where(left, high, turned(low))
                odd = jnp.where(left, turned(high), low)
                both = jnp.concatenate([even, odd], axis=0).astype(BF16)
                factor = w_ref[window]
                q_high = factor[0:BS]
                q_low = factor[BS : 2 * BS]
                products.append(
                    jnp.dot(
                        jnp.concatenate([both, both], axis=1),
                        jnp.concatenate([q_high, q_high, q_low, q_low], axis=0),
                        preferred_element_type=F32,
                    )
                )
            wide = jnp.concatenate(
                [
                    jnp.where(left_tall, products[0], products[1]),
                    jnp.where(left_tall, products[2], products[3]),
                ],
                axis=1,
            )
            high, low = split(wide)
            factor = t_ref[row]
            results.append(
                jnp.dot(
                    jnp.concatenate([factor, factor], axis=1),
                    jnp.concatenate([high, high, low, low], axis=0),
                    preferred_element_type=F32,
                )
            )
        for lane in range(GROUP):
            for pair in range(2):
                even = results[lane][0:PACK, pair * LANES : (pair + 1) * LANES]
                odd = results[lane][PACK:BS, pair * LANES : (pair + 1) * LANES]
                packed = [jnp.where(left, even, turned(odd)), jnp.where(left, turned(even), odd)]
                for k in range(2):
                    valid, place = places[lane * NNZ + pair * 2 + k]
                    where = pl.ds(pl.multiple_of(place * PACK, PACK), PACK)
                    out_ref[where, :] = out_ref[where, :] + jnp.where(valid, packed[k], 0.0)
        return used, labels

    used, labels = lax.fori_loop(0, groups, main, (zero, jnp.zeros((LABEL_ROWS, LANES), F32)))
    held = jnp.clip(used - base, 0, capacity)
    out_ref[pl.ds(capacity * PACK, LABEL_ROWS), :] = jnp.where(
        flat == LABEL_ROWS * LANES - 1, held.astype(F32), labels
    )
    used_ref[0] = used


def place_kernel(counts, capacity, home_count, clear, me_ref, *refs):
    own_count, partner_count = counts
    sources = refs[: own_count + partner_count]
    out_ref, token_ref, labels, zeros, label_sem, zero_sem, sem = refs[-7:]
    token_ref[0] = 0
    slots, row_groups = out_ref.shape[0], out_ref.shape[1]
    copies = []
    for which, source in enumerate(sources):
        copies.append(
            pltpu.make_async_copy(
                source.at[pl.ds(capacity * PACK, LABEL_ROWS)], labels.at[which], label_sem.at[which]
            )
        )
        copies[-1].start()
    if clear:
        zeros[...] = jnp.zeros_like(zeros)

        @pl.loop(0, slots)
        def _(slot):
            @pl.loop(0, row_groups)
            def _(group):
                pltpu.make_async_copy(zeros, out_ref.at[slot, group], zero_sem).start()

        @pl.loop(0, slots * row_groups)
        def _(step):
            pltpu.make_async_copy(zeros, out_ref.at[0, 0], zero_sem).wait()

    moved = jnp.int32(0)
    for which, source in enumerate(sources):
        copies[which].wait()
        upper = me_ref[2] if which < own_count else 1 - me_ref[2]
        held = labels[which, LABEL_ROWS - 1, 0, LANES - 1].astype(jnp.int32)

        @pl.loop(0, held)
        def _(place):
            label = labels[which, place // LANES, 0, place % LANES].astype(jnp.int32)
            slot = label // 2**ROW_BITS
            row = label % 2**ROW_BITS + upper * home_count
            pltpu.make_async_copy(
                source.at[pl.ds(place * PACK, PACK)], out_ref.at[slot, row // 8, :, row % 8], sem
            ).start()

        moved = moved + held

    @pl.loop(0, moved)
    def _(step):
        pltpu.make_async_copy(sources[0].at[pl.ds(0, PACK)], out_ref.at[0, 0, :, 0], sem).wait()


def placed_into(out, out_type, me, capacity, home_count, token, own, partner):
    sources = [value.reshape(-1, 1, LANES) for value in own + partner]
    clear = out is None
    return pl.pallas_call(
        functools.partial(place_kernel, (len(own), len(partner)), capacity, home_count, clear),
        in_specs=[SMEM] + [ANY] * len(sources) + [ANY if clear else HBM],
        out_specs=[HBM, SMEM],
        out_shape=[out_type, jax.ShapeDtypeStruct((1,), jnp.int32)],
        input_output_aliases={} if clear else {len(sources) + 1: 0},
        scratch_shapes=[
            pltpu.SMEM((len(sources), LABEL_ROWS, 1, LANES), F32),
            pltpu.VMEM((PACK, 8, 1, LANES), F32),
            pltpu.SemaphoreType.DMA((len(sources),)),
            pltpu.SemaphoreType.DMA,
            pltpu.SemaphoreType.DMA,
        ],
        compiler_params=pltpu.CompilerParams(vmem_limit_bytes=32 * 2**20),
        cost_estimate=SMALL,
    )(me, *sources, token if clear else out)


def gate_kernel(value_ref, token_ref, out_ref):
    pass


def gate(value, token):
    return pl.pallas_call(
        gate_kernel,
        in_specs=[ANY, ANY],
        out_specs=ANY,
        out_shape=jax.ShapeDtypeStruct(value.shape, value.dtype),
        input_output_aliases={0: 0},
        cost_estimate=SMALL,
    )(value, token)


def body(blocks, prolong, columns, aggregate, column_slot, owner_row):
    fine_rows = blocks.shape[0]
    home_count = owner_row.shape[0]
    size_gx = lax.axis_size("gx")
    size_gy = lax.axis_size("gy")
    size = size_gx * size_gy
    axes = ("gx", "gy")
    here_gx = lax.axis_index("gx")
    here_gy = lax.axis_index("gy")
    position = lax.axis_index(axes)
    bucket_rows = home_count // size_gx + 1
    most = bucket_rows * ROW_BLOCKS
    capacity = bucket_rows * FIRST_ROUND // 2
    most_fine = -(-bucket_rows * MOST_FINE // GROUP) * GROUP
    me = jnp.stack([here_gx, position, here_gy % 2]).astype(jnp.int32)

    block_view = (
        blocks.reshape(fine_rows, NNZ, PACK, LANES).transpose(0, 2, 1, 3).reshape(fine_rows, NNZ * PACK, LANES)
    )
    q_view = (
        prolong.reshape(fine_rows // 8, 8, PACK, LANES).transpose(0, 2, 1, 3).reshape(fine_rows * PACK, LANES)
    )
    group_rows = 8 * PACK
    backward = [(i, (i - 1) % size) for i in range(size)]
    forward = [(i, (i + 1) % size) for i in range(size)]
    edge_ints = jnp.concatenate(
        [columns.T[:, :2].reshape(-1), column_slot.T[:, :2].reshape(-1), aggregate[:2]]
    )
    edge_ints = lax.ppermute(edge_ints, axes, backward)
    after = lax.ppermute(q_view[:group_rows], axes, backward)
    edge_blocks = lax.ppermute(block_view[:2], axes, backward)
    before = lax.ppermute(q_view[-group_rows:], axes, forward)

    factor_types = [
        jax.ShapeDtypeStruct((fine_rows + BEFORE + AFTER, 2 * BS, LANES), BF16),
        jax.ShapeDtypeStruct((fine_rows + 2, BS, LANES), BF16),
    ]
    right, left = pl.pallas_call(
        functools.partial(prepare_kernel, fine_rows),
        in_specs=[VMEM],
        out_specs=[VMEM] * 2,
        out_shape=factor_types,
        scratch_shapes=[pltpu.VMEM((8, BS, LANES), F32), pltpu.VMEM((8, BS, LANES), F32)],
        compiler_params=pltpu.CompilerParams(vmem_limit_bytes=32 * 2**20),
        cost_estimate=cost_of(5e-6),
    )(q_view)
    right, left = pl.pallas_call(
        functools.partial(prepare_edge_kernel, fine_rows),
        in_specs=[VMEM] * 2 + [ANY] * 2,
        out_specs=[ANY] * 2,
        out_shape=factor_types,
        input_output_aliases={2: 0, 3: 1},
        scratch_shapes=[
            pltpu.VMEM((AFTER + BEFORE, 2 * BS, LANES), BF16),
            pltpu.VMEM((2, BS, LANES), BF16),
            pltpu.VMEM((AFTER + BEFORE, BS, LANES), F32),
            pltpu.VMEM((2, BS, LANES), F32),
            pltpu.SemaphoreType.DMA((3,)),
        ],
        compiler_params=pltpu.CompilerParams(vmem_limit_bytes=32 * 2**20),
        cost_estimate=SMALL,
    )(before, after, right, left)

    def bucket(shift, base, token):
        return pl.pallas_call(
            functools.partial(
                bucket_kernel,
                shift,
                base,
                capacity,
                fine_rows,
                fine_rows * size,
                home_count,
                home_count * size_gy,
            ),
            in_specs=[SMEM] * 6 + [ANY] * 2 + [VMEM] * 2 + [ANY],
            out_specs=[VMEM, SMEM],
            out_shape=[
                jax.ShapeDtypeStruct((capacity * PACK + LABEL_ROWS, LANES), F32),
                jax.ShapeDtypeStruct((1,), jnp.int32),
            ],
            scratch_shapes=[
                pltpu.VMEM((most_fine * 2 * BS, LANES), F32),
                pltpu.SMEM((most_fine + GROUP,), jnp.int32),
                pltpu.SMEM((most_fine + GROUP,), jnp.int32),
                pltpu.SMEM((most_fine + GROUP,), jnp.int32),
                pltpu.SMEM((bucket_rows * 8,), jnp.int32),
                pltpu.SemaphoreType.DMA,
            ],
            compiler_params=pltpu.CompilerParams(vmem_limit_bytes=40 * 2**20),
            cost_estimate=SMALL,
        )(
            me,
            columns.T,
            column_slot.T,
            aggregate,
            owner_row,
            edge_ints,
            block_view,
            edge_blocks,
            right,
            left,
            token,
        )

    def across(value, shift):
        pairs = [(source, source ^ shift) for source in range(size_gx)]
        return lax.ppermute(value, "gx", pairs)

    def partner(value):
        pairs = [(source, source ^ 1) for source in range(size_gy)]
        return lax.ppermute(value, "gy", pairs)

    def across_partner(value, shift):
        pairs = [
            (gx * size_gy + gy, (gx ^ shift) * size_gy + (gy ^ 1)) for gx in range(size_gx) for gy in range(size_gy)
        ]
        return lax.ppermute(value, axes, pairs)

    out_type = pltpu.HBM((SLOTS, 2 * home_count // 8, PACK, 8, 1, LANES), F32)

    def round_of(out, base):
        first = out is None
        own_sent, used = bucket(0, base, me)
        counts = [used]
        from_partner = {0: partner(own_sent)}
        sent = {0: own_sent}
        token = own_sent
        for shift in list(range(2, size_gx)) + [1]:
            sent[shift], used = bucket(shift, base, token)
            counts.append(used)
            token = sent[shift]
        if first:
            token = sent[1] = gate(sent[1], from_partner[0])
        from_partner[1] = across_partner(sent[1], 1)
        arrived = {shift: across(sent[shift], shift) for shift in range(1, size_gx)}
        place = functools.partial(
            placed_into, out_type=out_type, me=me, capacity=capacity, home_count=home_count, token=token
        )
        out, placed = place(out, own=[own_sent], partner=[from_partner[0]])
        for shift in range(2, size_gx):
            value = arrived[shift]
            if first and shift == 3:
                value = gate(value, placed)
            from_partner[shift] = partner(value)
        out, _ = place(out, own=[arrived[1]], partner=[from_partner[1]])
        out, _ = place(out, own=[arrived[2]], partner=[])
        for shift in range(3, size_gx):
            out, _ = place(out, own=[arrived[shift]], partner=[from_partner[shift - 1]])
        out, _ = place(out, own=[], partner=[from_partner[size_gx - 1]])
        return out, counts

    out, counts = round_of(None, 0)
    most_used = lax.pmax(functools.reduce(jnp.maximum, counts)[0], axes)
    for later in range(capacity, most, capacity):
        out = lax.cond(most_used > later, lambda out: round_of(out, later)[0], lambda out: out, out)
    return (
        out.reshape(SLOTS, 2 * home_count // 8, PACK, 8, LANES)
        .transpose(1, 3, 0, 2, 4)
        .reshape(2 * home_count, SLOTS, BS * BS)
    )


def solution(mesh):
    placed = (
        P(("gx", "gy"), None, None),
        P(("gx", "gy"), None),
        P(("gx", "gy"), None),
        P(("gx", "gy")),
        P(("gx", "gy"), None),
        P(("gx", "gy")),
    )
    return jax.shard_map(
        body, mesh=mesh, in_specs=placed, out_specs=P(("gx", "gy"), None, None), check_vma=False
    )
```

```python
import functools

import jax
import jax.numpy as jnp
from jax import lax
from jax.experimental import pallas as pl
from jax.experimental.pallas import tpu as pltpu
from jax.sharding import PartitionSpec as P

BS = 64
NNZ = 4
SLOTS = 7
ROW_BLOCKS = 6
MOST_FINE = 3
LANES = 128
PACK = BS * BS // LANES
BEFORE = 1
AFTER = 5
LABEL_ROWS = 8
GROUP = 4
ROW_BITS = 10
FIRST_ROUND = 9

F32 = jnp.float32
BF16 = jnp.bfloat16
ANY = pl.BlockSpec(memory_space=pl.ANY)
HBM = pl.BlockSpec(memory_space=pltpu.HBM)
SMEM = pl.BlockSpec(memory_space=pltpu.SMEM)
VMEM = pl.BlockSpec(memory_space=pltpu.VMEM)


def cost_of(seconds):
    return pl.CostEstimate(flops=int(seconds * 1e15), bytes_accessed=int(seconds * 3e12), transcendentals=0)


SMALL = cost_of(1e-6)


def half_lanes(shape):
    return lax.broadcasted_iota(jnp.int32, shape, 1) < LANES // 2


def turned(value):
    return pltpu.roll(value, LANES // 2, 1)


def split(value):
    high = value.astype(BF16)
    low = (value - high.astype(F32)).astype(BF16)
    return high, low


def halves(packed):
    left = half_lanes((PACK, LANES))
    swapped = turned(packed)
    return jnp.where(left, packed, swapped), jnp.where(left, swapped, packed)


def high_and_low(value):
    high, low = split(value)
    return jnp.where(half_lanes(value.shape), high.astype(F32), low.astype(F32)).astype(BF16)


def factor(packed, natural):
    even, odd = halves(packed)
    natural[pl.ds(0, PACK, stride=2), :] = even
    natural[pl.ds(1, PACK, stride=2), :] = odd
    return high_and_low(natural[...])


def transposed(packed, flipped):
    even, odd = halves(packed)
    flipped[...] = jnp.concatenate([even, odd, even, odd], axis=0).T[0:BS]
    return high_and_low(
        jnp.concatenate([flipped[pl.ds(0, PACK, stride=2), :], flipped[pl.ds(1, PACK, stride=2), :]], axis=0)
    )


def flat_index():
    shape = (LABEL_ROWS, LANES)
    return lax.broadcasted_iota(jnp.int32, shape, 0) * LANES + lax.broadcasted_iota(jnp.int32, shape, 1)


def edge_kernel(columns_ref, slots_ref, aggregate_ref, q_ref, blocks_ref, back_ref, forth_ref, sem):
    group_rows = 8 * PACK
    block_rows = NNZ * PACK
    copies = [
        pltpu.make_async_copy(q_ref.at[pl.ds(0, group_rows)], back_ref.at[pl.ds(0, group_rows)], sem.at[0]),
        pltpu.make_async_copy(
            q_ref.at[pl.ds(q_ref.shape[0] - group_rows, group_rows)], forth_ref, sem.at[1]
        ),
    ]
    for row in range(2):
        copies.append(
            pltpu.make_async_copy(
                blocks_ref.at[row], back_ref.at[pl.ds(group_rows + row * block_rows, block_rows)], sem.at[2 + row]
            )
        )
    for copy in copies:
        copy.start()
    flat = flat_index()
    values = [ref[k, row] for ref in (columns_ref, slots_ref) for k in range(NNZ) for row in range(2)]
    numbers = jnp.zeros((LABEL_ROWS, LANES), jnp.int32)
    for place, value in enumerate(values + [aggregate_ref[0], aggregate_ref[1]]):
        numbers = jnp.where(flat == place, value, numbers)
    back_ref[pl.ds(group_rows + 2 * block_rows, LABEL_ROWS), :] = numbers.astype(F32)
    for copy in copies:
        copy.wait()


def prepare_kernel(
    fine_rows, rows_of_gx, size_gx, slots_ref, aggregate_ref, owner_ref, q_ref, w_ref, bound_ref, natural
):
    def ones(mask):
        mask = mask - ((mask >> 1) & 0x55)
        mask = (mask & 0x33) + ((mask >> 2) & 0x33)
        return (mask + (mask >> 4)) & 0xF

    def blocks_of(pair, counts):
        rows = [jnp.minimum(pair * 4 + 2 + step, fine_rows - 1) for step in range(4)]
        masks = []
        for row in rows:
            mask = jnp.int32(0)
            for k in range(NNZ):
                mask = mask | (jnp.int32(1) << slots_ref[k, row])
            masks.append(mask)
        leading = aggregate_ref[rows[0]]
        second = aggregate_ref[rows[1]] == leading
        third = aggregate_ref[rows[2]] == leading
        merged = [
            masks[0] | jnp.where(second, masks[1], 0) | jnp.where(third, masks[2], 0),
            masks[3] | jnp.where(second, 0, masks[1]) | jnp.where(third, 0, masks[2]),
        ]
        counts = list(counts)
        for which in range(2):
            number = jnp.where(pair * 4 + 5 < fine_rows, ones(merged[which]), SLOTS)
            owner = owner_ref[pair * 2 + which]
            for gx in range(size_gx):
                there = (owner >= gx * rows_of_gx) & (owner < (gx + 1) * rows_of_gx)
                counts[gx] = counts[gx] + jnp.where(there, number, 0)
        return tuple(counts)

    def eight_rows(group, counts):
        for lane in range(8):
            packed = q_ref[pl.ds(group * (8 * PACK) + lane, PACK, stride=8), :]
            w_ref[group * 8 + lane + BEFORE] = factor(packed, natural.at[lane])
        return blocks_of(group * 2 + 1, blocks_of(group * 2, counts))

    counts = lax.fori_loop(0, fine_rows // 8, eight_rows, (jnp.int32(0),) * size_gx)
    bound_ref[...] = jnp.full(bound_ref.shape, functools.reduce(jnp.maximum, counts).astype(F32))


def prepare_edge_kernel(fine_rows, before_ref, edge_ref, w_in, w_ref, w_edge, natural, sem):
    for row in range(AFTER + BEFORE):
        source, base = (before_ref, 7) if row == AFTER else (edge_ref, row)
        w_edge[row] = factor(source[pl.ds(base, PACK, stride=8), :], natural.at[row])
    copies = [
        pltpu.make_async_copy(w_edge.at[pl.ds(0, AFTER)], w_ref.at[pl.ds(fine_rows + BEFORE, AFTER)], sem.at[0]),
        pltpu.make_async_copy(w_edge.at[pl.ds(AFTER, BEFORE)], w_ref.at[pl.ds(0, BEFORE)], sem.at[1]),
    ]
    for copy in copies:
        copy.start()
    for copy in copies:
        copy.wait()


def bucket_kernel(
    shift,
    base,
    capacity,
    fine_rows,
    fine_total,
    home_count,
    rows_of_gx,
    me_ref,
    columns_ref,
    slots_ref,
    aggregate_ref,
    owner_ref,
    blocks_ref,
    numbers_ref,
    edge_ref,
    q_ref,
    w_ref,
    token_ref,
    other_ref,
    out_ref,
    stored,
    flipped,
    numbers,
    edge_list,
    fine_list,
    table_list,
    local_list,
    place_of,
    in_sem,
    number_sem,
):
    lowest = (me_ref[0] ^ shift) * rows_of_gx
    first_block = me_ref[1] * fine_rows
    flat = flat_index()
    block_rows = NNZ * PACK
    edge_base = 8 * PACK
    number_copy = pltpu.make_async_copy(
        numbers_ref.at[pl.ds(edge_base + 2 * block_rows, LABEL_ROWS)], numbers, number_sem
    )
    number_copy.start()

    def listing(pair, groups, carry):
        listed, tables, own = carry
        start = pair * 4 + 2
        size = 1 + (groups[1] == groups[0]).astype(jnp.int32) + (groups[2] == groups[0]).astype(jnp.int32)
        owners = [owner_ref[pair * 2], owner_ref[pair * 2 + 1]]
        match = [((owner >= lowest) & (owner < lowest + rows_of_gx)).astype(jnp.int32) for owner in owners]
        local = [lax.rem(owner, home_count) for owner in owners]
        table = [tables, tables + match[0]]
        for step in range(4):
            second = size <= step
            fine_list[listed] = start + step
            table_list[listed] = jnp.where(second, table[1], table[0]) * 8
            local_list[listed] = jnp.where(second, local[1], local[0])
            listed = listed + jnp.where(second, match[1], match[0])
            own = jnp.where(start + step < fine_rows, listed, own)
        return listed, tables + match[0] + match[1], own

    zero = jnp.int32(0)
    last = home_count // 2 - 1
    carry = lax.fori_loop(
        0,
        last,
        lambda pair, carry: listing(pair, [aggregate_ref[pair * 4 + 2 + step] for step in range(3)], carry),
        (zero, zero, zero),
    )
    number_copy.wait()
    for place in range(4 * NNZ + 1):
        edge_list[place] = numbers[0, 0, place].astype(jnp.int32)
    edge_groups = [aggregate_ref[last * 4 + 2], aggregate_ref[last * 4 + 3], edge_list[4 * NNZ]]
    listed, tables, own = listing(last, edge_groups, carry)

    def target(index):
        return stored.at[pl.ds(pl.multiple_of(index * 2 * BS, 2 * BS), 2 * BS)]

    @pl.loop(0, own)
    def _(index):
        pltpu.make_async_copy(blocks_ref.at[fine_list[index]], target(index), in_sem).start()

    @pl.loop(own, listed)
    def _(index):
        first = edge_base + (fine_list[index] - fine_rows) * block_rows
        source = edge_ref.at[pl.ds(pl.multiple_of(first, block_rows), block_rows)]
        pltpu.make_async_copy(source, target(index), in_sem).start()

    @pl.loop(0, tables)
    def _(table):
        for slot in range(SLOTS):
            place_of[table * 8 + slot] = -1

    @pl.loop(0, capacity)
    def _(place):
        out_ref[pl.ds(pl.multiple_of(place * PACK, PACK), PACK), :] = jnp.zeros((PACK, LANES), F32)

    groups = (listed + GROUP - 1) // GROUP

    @pl.loop(listed, groups * GROUP)
    def _(index):
        fine_list[index] = 2
        table_list[index] = 0
        local_list[index] = 0

    @pl.loop(0, listed)
    def _(index):
        pltpu.make_async_copy(blocks_ref.at[0], target(0), in_sem).wait()

    left = half_lanes((PACK, LANES))
    left_tall = half_lanes((BS, LANES))

    def main(group, carry):
        used, labels = carry
        results = []
        places = []
        for lane in range(GROUP):
            index = group * GROUP + lane
            real = index < listed
            row = fine_list[index]
            inside = row < fine_rows
            own_row = jnp.where(inside, row, 0)
            edge_row = jnp.where(inside, 0, row - fine_rows)
            products = []
            for k in range(NNZ):
                column = jnp.where(inside, columns_ref[k, own_row], edge_list[k * 2 + edge_row])
                window = column - first_block + BEFORE
                window = jnp.where(window < 0, window + fine_total, window)
                window = jnp.where(window >= fine_total, window - fine_total, window)
                slot = jnp.where(inside, slots_ref[k, own_row], edge_list[2 * NNZ + k * 2 + edge_row])
                entry = table_list[index] + slot
                seen = place_of[entry]
                new = (seen < 0) & real
                place = jnp.where(new, used, seen)
                place_of[entry] = place
                used = used + new.astype(jnp.int32)
                valid = real & (place >= base) & (place < base + capacity)
                place = jnp.where(valid, place - base, 0)
                places.append((valid, place))
                label = (slot * 2**ROW_BITS + local_list[index]).astype(F32)
                labels = jnp.where((flat == place) & valid, label, labels)
                packed = stored[pl.ds(index * 2 * BS + k, PACK, stride=NNZ), :]
                high = packed.astype(BF16).astype(F32)
                low = packed - high
                even = jnp.where(left, high, turned(low))
                odd = jnp.where(left, turned(high), low)
                both = jnp.concatenate([even, odd], axis=0).astype(BF16)
                right = w_ref[window]
                parts = jnp.dot(both, jnp.concatenate([right, right], axis=0), preferred_element_type=F32)
                products.append(parts + turned(parts))
            wide = jnp.concatenate(
                [
                    jnp.where(left_tall, products[0], products[1]),
                    jnp.where(left_tall, products[2], products[3]),
                ],
                axis=1,
            )
            high, low = split(wide)
            mine = q_ref[pl.ds((own_row // 8) * (8 * PACK) + own_row % 8, PACK, stride=8), :]
            other = edge_ref[pl.ds(edge_row, PACK, stride=8), :]
            row = transposed(jnp.where(inside, mine, other), flipped.at[lane])
            results.append(
                jnp.dot(
                    jnp.concatenate([row, row[:, 0:BS]], axis=1),
                    jnp.concatenate([high, high, low], axis=0),
                    preferred_element_type=F32,
                )
            )
        for lane in range(GROUP):
            for pair in range(2):
                even = results[lane][0:PACK, pair * LANES : (pair + 1) * LANES]
                odd = results[lane][PACK:BS, pair * LANES : (pair + 1) * LANES]
                packed = [jnp.where(left, even, turned(odd)), jnp.where(left, turned(even), odd)]
                for k in range(2):
                    valid, place = places[lane * NNZ + pair * 2 + k]
                    where = pl.ds(pl.multiple_of(place * PACK, PACK), PACK)
                    out_ref[where, :] = out_ref[where, :] + jnp.where(valid, packed[k], 0.0)
        return used, labels

    used, labels = lax.fori_loop(0, groups, main, (zero, jnp.zeros((LABEL_ROWS, LANES), F32)))
    held = jnp.clip(used - base, 0, capacity)
    out_ref[pl.ds(capacity * PACK, LABEL_ROWS), :] = jnp.where(
        flat == LABEL_ROWS * LANES - 1, held.astype(F32), labels
    )


def place_kernel(counts, capacity, home_count, clear, me_ref, *refs):
    own_count, partner_count = counts
    sources = refs[: own_count + partner_count]
    out_ref, token_ref, labels, zeros, label_sem, zero_sem, sem = refs[-7:]
    token_ref[0] = 0
    slots, row_groups = out_ref.shape[0], out_ref.shape[1]
    copies = []
    for which, source in enumerate(sources):
        copies.append(
            pltpu.make_async_copy(
                source.at[pl.ds(capacity * PACK, LABEL_ROWS)], labels.at[which], label_sem.at[which]
            )
        )
        copies[-1].start()
    if clear:
        zeros[...] = jnp.zeros_like(zeros)

        @pl.loop(0, slots)
        def _(slot):
            @pl.loop(0, row_groups)
            def _(group):
                pltpu.make_async_copy(zeros, out_ref.at[slot, group], zero_sem).start()

        @pl.loop(0, slots * row_groups)
        def _(step):
            pltpu.make_async_copy(zeros, out_ref.at[0, 0], zero_sem).wait()

    moved = jnp.int32(0)
    for which, source in enumerate(sources):
        copies[which].wait()
        upper = me_ref[2] if which < own_count else 1 - me_ref[2]
        held = labels[which, LABEL_ROWS - 1, 0, LANES - 1].astype(jnp.int32)

        @pl.loop(0, held)
        def _(place):
            label = labels[which, place // LANES, 0, place % LANES].astype(jnp.int32)
            slot = label // 2**ROW_BITS
            row = label % 2**ROW_BITS + upper * home_count
            pltpu.make_async_copy(
                source.at[pl.ds(place * PACK, PACK)], out_ref.at[slot, row // 8, :, row % 8], sem
            ).start()

        moved = moved + held

    @pl.loop(0, moved)
    def _(step):
        pltpu.make_async_copy(sources[0].at[pl.ds(0, PACK)], out_ref.at[0, 0, :, 0], sem).wait()


def placed_into(out, out_type, me, capacity, home_count, token, own, partner):
    sources = [value.reshape(-1, 1, LANES) for value in own + partner]
    clear = out is None
    return pl.pallas_call(
        functools.partial(place_kernel, (len(own), len(partner)), capacity, home_count, clear),
        in_specs=[SMEM] + [VMEM] * len(sources) + [ANY if clear else HBM],
        out_specs=[HBM, SMEM],
        out_shape=[out_type, jax.ShapeDtypeStruct((1,), jnp.int32)],
        input_output_aliases={} if clear else {len(sources) + 1: 0},
        scratch_shapes=[
            pltpu.SMEM((len(sources), LABEL_ROWS, 1, LANES), F32),
            pltpu.VMEM((PACK, 8, 1, LANES), F32),
            pltpu.SemaphoreType.DMA((len(sources),)),
            pltpu.SemaphoreType.DMA,
            pltpu.SemaphoreType.DMA,
        ],
        compiler_params=pltpu.CompilerParams(vmem_limit_bytes=32 * 2**20),
        cost_estimate=SMALL,
    )(me, *sources, token if clear else out)


def gate_kernel(value_ref, token_ref, out_ref):
    out_ref[...] = value_ref[...]


def gate(value, token):
    return pl.pallas_call(
        gate_kernel,
        in_specs=[VMEM, ANY],
        out_specs=VMEM,
        out_shape=jax.ShapeDtypeStruct(value.shape, value.dtype),
        compiler_params=pltpu.CompilerParams(vmem_limit_bytes=24 * 2**20),
        cost_estimate=SMALL,
    )(value, token)


def most_kernel(bounds_ref, token_ref, most_ref):
    most_ref[0] = jnp.max(bounds_ref[...]).astype(jnp.int32)


def body(blocks, prolong, columns, aggregate, column_slot, owner_row):
    fine_rows = blocks.shape[0]
    home_count = owner_row.shape[0]
    size_gx = lax.axis_size("gx")
    size_gy = lax.axis_size("gy")
    size = size_gx * size_gy
    axes = ("gx", "gy")
    here_gx = lax.axis_index("gx")
    here_gy = lax.axis_index("gy")
    position = lax.axis_index(axes)
    bucket_rows = home_count // size_gx + 1
    most = bucket_rows * ROW_BLOCKS
    capacity = bucket_rows * FIRST_ROUND // 2
    most_fine = -(-bucket_rows * MOST_FINE // GROUP) * GROUP
    me = jnp.stack([here_gx, position, here_gy % 2]).astype(jnp.int32)

    block_view = (
        blocks.reshape(fine_rows, NNZ, PACK, LANES).transpose(0, 2, 1, 3).reshape(fine_rows, NNZ * PACK, LANES)
    )
    q_view = (
        prolong.reshape(fine_rows // 8, 8, PACK, LANES).transpose(0, 2, 1, 3).reshape(fine_rows * PACK, LANES)
    )
    edge_rows = 8 * PACK + 2 * NNZ * PACK + LABEL_ROWS
    backward = [(i, (i - 1) % size) for i in range(size)]
    forward = [(i, (i + 1) % size) for i in range(size)]
    back, forth = pl.pallas_call(
        edge_kernel,
        in_specs=[SMEM] * 3 + [ANY] * 2,
        out_specs=[VMEM] * 2,
        out_shape=[
            jax.ShapeDtypeStruct((edge_rows, LANES), F32),
            jax.ShapeDtypeStruct((8 * PACK, LANES), F32),
        ],
        scratch_shapes=[pltpu.SemaphoreType.DMA((4,))],
        compiler_params=pltpu.CompilerParams(vmem_limit_bytes=48 * 2**20),
        cost_estimate=SMALL,
    )(columns.T, column_slot.T, aggregate, q_view, block_view)
    edge = lax.ppermute(back, axes, backward)
    before = lax.ppermute(forth, axes, forward)

    factor_type = jax.ShapeDtypeStruct((fine_rows + BEFORE + AFTER, BS, LANES), BF16)
    right, bound = pl.pallas_call(
        functools.partial(prepare_kernel, fine_rows, home_count * size_gy, size_gx),
        in_specs=[SMEM] * 3 + [VMEM],
        out_specs=[VMEM] * 2,
        out_shape=[factor_type, jax.ShapeDtypeStruct((8, LANES), F32)],
        scratch_shapes=[pltpu.VMEM((8, BS, LANES), F32)],
        compiler_params=pltpu.CompilerParams(vmem_limit_bytes=32 * 2**20),
        cost_estimate=cost_of(5e-6),
    )(column_slot.T, aggregate, owner_row, q_view)
    bounds = lax.all_gather(bound, axes, tiled=True)
    right = pl.pallas_call(
        functools.partial(prepare_edge_kernel, fine_rows),
        in_specs=[VMEM] * 2 + [ANY],
        out_specs=ANY,
        out_shape=factor_type,
        input_output_aliases={2: 0},
        scratch_shapes=[
            pltpu.VMEM((AFTER + BEFORE, BS, LANES), BF16),
            pltpu.VMEM((AFTER + BEFORE, BS, LANES), F32),
            pltpu.SemaphoreType.DMA((2,)),
        ],
        compiler_params=pltpu.CompilerParams(vmem_limit_bytes=32 * 2**20),
        cost_estimate=SMALL,
    )(before, edge, right)

    def bucket(shift, base, token, other):
        return pl.pallas_call(
            functools.partial(
                bucket_kernel,
                shift,
                base,
                capacity,
                fine_rows,
                fine_rows * size,
                home_count,
                home_count * size_gy,
            ),
            in_specs=[SMEM] * 5 + [ANY] * 2 + [VMEM] * 3 + [ANY] * 2,
            out_specs=VMEM,
            out_shape=jax.ShapeDtypeStruct((capacity * PACK + LABEL_ROWS, LANES), F32),
            scratch_shapes=[
                pltpu.VMEM((most_fine * 2 * BS, LANES), F32),
                pltpu.VMEM((GROUP, BS, LANES), F32),
                pltpu.SMEM((LABEL_ROWS, 1, LANES), F32),
                pltpu.SMEM((4 * NNZ + 2,), jnp.int32),
                pltpu.SMEM((most_fine + GROUP,), jnp.int32),
                pltpu.SMEM((most_fine + GROUP,), jnp.int32),
                pltpu.SMEM((most_fine + GROUP,), jnp.int32),
                pltpu.SMEM((bucket_rows * 8,), jnp.int32),
                pltpu.SemaphoreType.DMA,
                pltpu.SemaphoreType.DMA,
            ],
            compiler_params=pltpu.CompilerParams(vmem_limit_bytes=40 * 2**20),
            cost_estimate=SMALL,
        )(
            me,
            columns.T,
            column_slot.T,
            aggregate,
            owner_row,
            block_view,
            edge.reshape(-1, 1, LANES),
            edge,
            q_view,
            right,
            token,
            other,
        )

    def across(value, shift):
        pairs = [(source, source ^ shift) for source in range(size_gx)]
        return lax.ppermute(value, "gx", pairs)

    def partner(value):
        pairs = [(source, source ^ 1) for source in range(size_gy)]
        return lax.ppermute(value, "gy", pairs)

    def across_partner(value, shift):
        pairs = [
            (gx * size_gy + gy, (gx ^ shift) * size_gy + (gy ^ 1)) for gx in range(size_gx) for gy in range(size_gy)
        ]
        return lax.ppermute(value, axes, pairs)

    out_type = pltpu.HBM((SLOTS, 2 * home_count // 8, PACK, 8, 1, LANES), F32)

    def round_of(out, base):
        first = out is None
        own_sent = bucket(0, base, me, me)
        from_partner = {0: partner(own_sent)}
        sent = {0: own_sent}
        token = own_sent
        for shift in [2, 1] + list(range(3, size_gx)):
            sent[shift] = bucket(shift, base, token, bounds if first and shift == 3 else me)
            if first and shift == 1:
                sent[1] = gate(sent[1], from_partner[0])
            token = sent[shift]
        from_partner[1] = across_partner(sent[1], 1)
        arrived = {shift: across(sent[shift], shift) for shift in range(1, size_gx)}
        place = functools.partial(
            placed_into, out_type=out_type, me=me, capacity=capacity, home_count=home_count, token=token
        )
        out, placed = place(out, own=[own_sent], partner=[from_partner[0]])
        for shift in range(2, size_gx):
            value = arrived[shift]
            if first and shift < 4:
                value = gate(value, from_partner[1] if shift == 2 else placed)
            from_partner[shift] = partner(value)
        out, _ = place(out, own=[arrived[1]], partner=[from_partner[1]])
        out, _ = place(out, own=[arrived[2]], partner=[])
        for shift in range(3, size_gx):
            out, placed = place(out, own=[arrived[shift]], partner=[from_partner[shift - 1]])
        out, _ = place(out, own=[], partner=[from_partner[size_gx - 1]])
        return out, placed

    out, token = round_of(None, 0)
    most_used = pl.pallas_call(
        most_kernel,
        in_specs=[VMEM, SMEM],
        out_specs=SMEM,
        out_shape=jax.ShapeDtypeStruct((1,), jnp.int32),
        cost_estimate=SMALL,
    )(bounds, token)[0]
    for later in range(capacity, most, capacity):
        out = lax.cond(most_used > later, lambda out: round_of(out, later)[0], lambda out: out, out)
    return (
        out.reshape(SLOTS, 2 * home_count // 8, PACK, 8, LANES)
        .transpose(1, 3, 0, 2, 4)
        .reshape(2 * home_count, SLOTS, BS * BS)
    )


def solution(mesh):
    placed = (
        P(("gx", "gy"), None, None),
        P(("gx", "gy"), None),
        P(("gx", "gy"), None),
        P(("gx", "gy")),
        P(("gx", "gy"), None),
        P(("gx", "gy")),
    )
    return jax.shard_map(
        body, mesh=mesh, in_specs=placed, out_specs=P(("gx", "gy"), None, None), check_vma=False
    )
```

```python
import functools

import jax
import jax.numpy as jnp
from jax import lax
from jax.experimental import pallas as pl
from jax.experimental.pallas import tpu as pltpu
from jax.sharding import PartitionSpec as P

BS = 64
NNZ = 4
SLOTS = 7
ROW_BLOCKS = 6
MOST_FINE = 3
LANES = 128
PACK = BS * BS // LANES
BEFORE = 1
AFTER = 5
LABEL_ROWS = 8
GROUP = 4
ROW_BITS = 10
FIRST_ROUND = 9

F32 = jnp.float32
BF16 = jnp.bfloat16
ANY = pl.BlockSpec(memory_space=pl.ANY)
HBM = pl.BlockSpec(memory_space=pltpu.HBM)
SMEM = pl.BlockSpec(memory_space=pltpu.SMEM)
VMEM = pl.BlockSpec(memory_space=pltpu.VMEM)


def cost_of(seconds):
    return pl.CostEstimate(flops=int(seconds * 1e15), bytes_accessed=int(seconds * 3e12), transcendentals=0)


SMALL = cost_of(1e-6)


def half_lanes(shape):
    return lax.broadcasted_iota(jnp.int32, shape, 1) < LANES // 2


def turned(value):
    return pltpu.roll(value, LANES // 2, 1)


def split(value):
    high = value.astype(BF16)
    low = (value - high.astype(F32)).astype(BF16)
    return high, low


def halves(packed):
    left = half_lanes((PACK, LANES))
    swapped = turned(packed)
    return jnp.where(left, packed, swapped), jnp.where(left, swapped, packed)


def high_and_low(value):
    high, low = split(value)
    return jnp.where(half_lanes(value.shape), high.astype(F32), low.astype(F32)).astype(BF16)


def factor(packed, natural):
    even, odd = halves(packed)
    natural[pl.ds(0, PACK, stride=2), :] = even
    natural[pl.ds(1, PACK, stride=2), :] = odd
    return high_and_low(natural[...])


def transposed(packed, flipped):
    even, odd = halves(packed)
    flipped[...] = jnp.concatenate([even, odd, even, odd], axis=0).T[0:BS]
    return high_and_low(
        jnp.concatenate([flipped[pl.ds(0, PACK, stride=2), :], flipped[pl.ds(1, PACK, stride=2), :]], axis=0)
    )


def flat_index():
    shape = (LABEL_ROWS, LANES)
    return lax.broadcasted_iota(jnp.int32, shape, 0) * LANES + lax.broadcasted_iota(jnp.int32, shape, 1)


def edge_kernel(columns_ref, slots_ref, aggregate_ref, q_ref, blocks_ref, back_ref, forth_ref, sem):
    group_rows = 8 * PACK
    block_rows = NNZ * PACK
    copies = [
        pltpu.make_async_copy(q_ref.at[pl.ds(0, group_rows)], back_ref.at[pl.ds(0, group_rows)], sem.at[0]),
        pltpu.make_async_copy(
            q_ref.at[pl.ds(q_ref.shape[0] - group_rows, group_rows)], forth_ref, sem.at[1]
        ),
    ]
    for row in range(2):
        copies.append(
            pltpu.make_async_copy(
                blocks_ref.at[row], back_ref.at[pl.ds(group_rows + row * block_rows, block_rows)], sem.at[2 + row]
            )
        )
    for copy in copies:
        copy.start()
    flat = flat_index()
    values = [ref[k, row] for ref in (columns_ref, slots_ref) for k in range(NNZ) for row in range(2)]
    numbers = jnp.zeros((LABEL_ROWS, LANES), jnp.int32)
    for place, value in enumerate(values + [aggregate_ref[0], aggregate_ref[1]]):
        numbers = jnp.where(flat == place, value, numbers)
    back_ref[pl.ds(group_rows + 2 * block_rows, LABEL_ROWS), :] = numbers.astype(F32)
    for copy in copies:
        copy.wait()


def prepare_kernel(
    fine_rows, rows_of_gx, size_gx, slots_ref, aggregate_ref, owner_ref, q_ref, w_ref, bound_ref, natural
):
    def ones(mask):
        mask = mask - ((mask >> 1) & 0x55)
        mask = (mask & 0x33) + ((mask >> 2) & 0x33)
        return (mask + (mask >> 4)) & 0xF

    def blocks_of(pair, counts):
        rows = [jnp.minimum(pair * 4 + 2 + step, fine_rows - 1) for step in range(4)]
        masks = []
        for row in rows:
            mask = jnp.int32(0)
            for k in range(NNZ):
                mask = mask | (jnp.int32(1) << slots_ref[k, row])
            masks.append(mask)
        leading = aggregate_ref[rows[0]]
        second = aggregate_ref[rows[1]] == leading
        third = aggregate_ref[rows[2]] == leading
        merged = [
            masks[0] | jnp.where(second, masks[1], 0) | jnp.where(third, masks[2], 0),
            masks[3] | jnp.where(second, 0, masks[1]) | jnp.where(third, 0, masks[2]),
        ]
        counts = list(counts)
        for which in range(2):
            number = jnp.where(pair * 4 + 5 < fine_rows, ones(merged[which]), SLOTS)
            owner = owner_ref[pair * 2 + which]
            for gx in range(size_gx):
                there = (owner >= gx * rows_of_gx) & (owner < (gx + 1) * rows_of_gx)
                counts[gx] = counts[gx] + jnp.where(there, number, 0)
        return tuple(counts)

    def eight_rows(group, counts):
        for lane in range(8):
            packed = q_ref[pl.ds(group * (8 * PACK) + lane, PACK, stride=8), :]
            w_ref[group * 8 + lane + BEFORE] = factor(packed, natural.at[lane])
        return blocks_of(group * 2 + 1, blocks_of(group * 2, counts))

    counts = lax.fori_loop(0, fine_rows // 8, eight_rows, (jnp.int32(0),) * size_gx)
    bound_ref[...] = jnp.full(bound_ref.shape, functools.reduce(jnp.maximum, counts).astype(F32))


def prepare_edge_kernel(fine_rows, before_ref, edge_ref, w_in, w_ref, w_edge, natural, sem):
    for row in range(AFTER + BEFORE):
        source, base = (before_ref, 7) if row == AFTER else (edge_ref, row)
        w_edge[row] = factor(source[pl.ds(base, PACK, stride=8), :], natural.at[row])
    copies = [
        pltpu.make_async_copy(w_edge.at[pl.ds(0, AFTER)], w_ref.at[pl.ds(fine_rows + BEFORE, AFTER)], sem.at[0]),
        pltpu.make_async_copy(w_edge.at[pl.ds(AFTER, BEFORE)], w_ref.at[pl.ds(0, BEFORE)], sem.at[1]),
    ]
    for copy in copies:
        copy.start()
    for copy in copies:
        copy.wait()


def bucket_kernel(
    shift,
    base,
    capacity,
    fine_rows,
    fine_total,
    home_count,
    rows_of_gx,
    me_ref,
    columns_ref,
    slots_ref,
    aggregate_ref,
    owner_ref,
    blocks_ref,
    numbers_ref,
    edge_ref,
    q_ref,
    w_ref,
    token_ref,
    other_ref,
    out_ref,
    stored,
    flipped,
    numbers,
    edge_list,
    fine_list,
    table_list,
    local_list,
    place_of,
    in_sem,
    number_sem,
):
    lowest = (me_ref[0] ^ shift) * rows_of_gx
    first_block = me_ref[1] * fine_rows
    flat = flat_index()
    block_rows = NNZ * PACK
    edge_base = 8 * PACK
    number_copy = pltpu.make_async_copy(
        numbers_ref.at[pl.ds(edge_base + 2 * block_rows, LABEL_ROWS)], numbers, number_sem
    )
    number_copy.start()

    def listing(pair, groups, carry):
        listed, tables, own = carry
        start = pair * 4 + 2
        size = 1 + (groups[1] == groups[0]).astype(jnp.int32) + (groups[2] == groups[0]).astype(jnp.int32)
        owners = [owner_ref[pair * 2], owner_ref[pair * 2 + 1]]
        match = [((owner >= lowest) & (owner < lowest + rows_of_gx)).astype(jnp.int32) for owner in owners]
        local = [lax.rem(owner, home_count) for owner in owners]
        table = [tables, tables + match[0]]
        for step in range(4):
            second = size <= step
            fine_list[listed] = start + step
            table_list[listed] = jnp.where(second, table[1], table[0]) * 8
            local_list[listed] = jnp.where(second, local[1], local[0])
            listed = listed + jnp.where(second, match[1], match[0])
            own = jnp.where(start + step < fine_rows, listed, own)
        return listed, tables + match[0] + match[1], own

    zero = jnp.int32(0)
    last = home_count // 2 - 1
    carry = lax.fori_loop(
        0,
        last,
        lambda pair, carry: listing(pair, [aggregate_ref[pair * 4 + 2 + step] for step in range(3)], carry),
        (zero, zero, zero),
    )
    number_copy.wait()
    for place in range(4 * NNZ + 1):
        edge_list[place] = numbers[0, 0, place].astype(jnp.int32)
    edge_groups = [aggregate_ref[last * 4 + 2], aggregate_ref[last * 4 + 3], edge_list[4 * NNZ]]
    listed, tables, own = listing(last, edge_groups, carry)

    def target(index):
        return stored.at[pl.ds(pl.multiple_of(index * 2 * BS, 2 * BS), 2 * BS)]

    @pl.loop(0, own)
    def _(index):
        pltpu.make_async_copy(blocks_ref.at[fine_list[index]], target(index), in_sem).start()

    @pl.loop(own, listed)
    def _(index):
        first = edge_base + (fine_list[index] - fine_rows) * block_rows
        source = edge_ref.at[pl.ds(pl.multiple_of(first, block_rows), block_rows)]
        pltpu.make_async_copy(source, target(index), in_sem).start()

    @pl.loop(0, tables)
    def _(table):
        for slot in range(SLOTS):
            place_of[table * 8 + slot] = -1

    @pl.loop(0, capacity)
    def _(place):
        out_ref[pl.ds(pl.multiple_of(place * PACK, PACK), PACK), :] = jnp.zeros((PACK, LANES), F32)

    groups = (listed + GROUP - 1) // GROUP

    @pl.loop(listed, groups * GROUP)
    def _(index):
        fine_list[index] = 2
        table_list[index] = 0
        local_list[index] = 0

    @pl.loop(0, listed)
    def _(index):
        pltpu.make_async_copy(blocks_ref.at[0], target(0), in_sem).wait()

    left = half_lanes((PACK, LANES))
    left_tall = half_lanes((BS, LANES))

    def main(group, carry):
        used, labels = carry
        results = []
        places = []
        for lane in range(GROUP):
            index = group * GROUP + lane
            real = index < listed
            row = fine_list[index]
            inside = row < fine_rows
            own_row = jnp.where(inside, row, 0)
            edge_row = jnp.where(inside, 0, row - fine_rows)
            products = []
            for k in range(NNZ):
                column = jnp.where(inside, columns_ref[k, own_row], edge_list[k * 2 + edge_row])
                window = column - first_block + BEFORE
                window = jnp.where(window < 0, window + fine_total, window)
                window = jnp.where(window >= fine_total, window - fine_total, window)
                slot = jnp.where(inside, slots_ref[k, own_row], edge_list[2 * NNZ + k * 2 + edge_row])
                entry = table_list[index] + slot
                seen = place_of[entry]
                new = (seen < 0) & real
                place = jnp.where(new, used, seen)
                place_of[entry] = place
                used = used + new.astype(jnp.int32)
                valid = real & (place >= base) & (place < base + capacity)
                place = jnp.where(valid, place - base, 0)
                places.append((valid, place))
                label = (slot * 2**ROW_BITS + local_list[index]).astype(F32)
                labels = jnp.where((flat == place) & valid, label, labels)
                packed = stored[pl.ds(index * 2 * BS + k, PACK, stride=NNZ), :]
                high = packed.astype(BF16).astype(F32)
                low = packed - high
                even = jnp.where(left, high, turned(low))
                odd = jnp.where(left, turned(high), low)
                both = jnp.concatenate([even, odd], axis=0).astype(BF16)
                right = w_ref[window]
                parts = jnp.dot(both, jnp.concatenate([right, right], axis=0), preferred_element_type=F32)
                products.append(parts + turned(parts))
            wide = jnp.concatenate(
                [
                    jnp.where(left_tall, products[0], products[1]),
                    jnp.where(left_tall, products[2], products[3]),
                ],
                axis=1,
            )
            high, low = split(wide)
            mine = q_ref[pl.ds((own_row // 8) * (8 * PACK) + own_row % 8, PACK, stride=8), :]
            other = edge_ref[pl.ds(edge_row, PACK, stride=8), :]
            row = transposed(jnp.where(inside, mine, other), flipped.at[lane])
            results.append(
                jnp.dot(
                    jnp.concatenate([row, row[:, 0:BS]], axis=1),
                    jnp.concatenate([high, high, low], axis=0),
                    preferred_element_type=F32,
                )
            )
        for lane in range(GROUP):
            for pair in range(2):
                even = results[lane][0:PACK, pair * LANES : (pair + 1) * LANES]
                odd = results[lane][PACK:BS, pair * LANES : (pair + 1) * LANES]
                packed = [jnp.where(left, even, turned(odd)), jnp.where(left, turned(even), odd)]
                for k in range(2):
                    valid, place = places[lane * NNZ + pair * 2 + k]
                    where = pl.ds(pl.multiple_of(place * PACK, PACK), PACK)
                    out_ref[where, :] = out_ref[where, :] + jnp.where(valid, packed[k], 0.0)
        return used, labels

    used, labels = lax.fori_loop(0, groups, main, (zero, jnp.zeros((LABEL_ROWS, LANES), F32)))
    held = jnp.clip(used - base, 0, capacity)
    out_ref[pl.ds(capacity * PACK, LABEL_ROWS), :] = jnp.where(
        flat == LABEL_ROWS * LANES - 1, held.astype(F32), labels
    )


def place_kernel(counts, capacity, home_count, clear, me_ref, *refs):
    own_count, partner_count = counts
    sources = refs[: own_count + partner_count]
    out_ref, token_ref, labels, zeros, label_sem, zero_sem, sem = refs[-7:]
    token_ref[0] = 0
    slots, row_groups = out_ref.shape[0], out_ref.shape[1]
    copies = []
    for which, source in enumerate(sources):
        copies.append(
            pltpu.make_async_copy(
                source.at[pl.ds(capacity * PACK, LABEL_ROWS)], labels.at[which], label_sem.at[which]
            )
        )
        copies[-1].start()
    if clear:
        zeros[...] = jnp.zeros_like(zeros)

        @pl.loop(0, slots)
        def _(slot):
            @pl.loop(0, row_groups)
            def _(group):
                pltpu.make_async_copy(zeros, out_ref.at[slot, group], zero_sem).start()

        @pl.loop(0, slots * row_groups)
        def _(step):
            pltpu.make_async_copy(zeros, out_ref.at[0, 0], zero_sem).wait()

    moved = jnp.int32(0)
    for which, source in enumerate(sources):
        copies[which].wait()
        upper = me_ref[2] if which < own_count else 1 - me_ref[2]
        held = labels[which, LABEL_ROWS - 1, 0, LANES - 1].astype(jnp.int32)

        @pl.loop(0, held)
        def _(place):
            label = labels[which, place // LANES, 0, place % LANES].astype(jnp.int32)
            slot = label // 2**ROW_BITS
            row = label % 2**ROW_BITS + upper * home_count
            pltpu.make_async_copy(
                source.at[pl.ds(place * PACK, PACK)], out_ref.at[slot, row // 8, :, row % 8], sem
            ).start()

        moved = moved + held

    @pl.loop(0, moved)
    def _(step):
        pltpu.make_async_copy(sources[0].at[pl.ds(0, PACK)], out_ref.at[0, 0, :, 0], sem).wait()


def placed_into(out, out_type, me, capacity, home_count, token, own, partner):
    sources = [value.reshape(-1, 1, LANES) for value in own + partner]
    clear = out is None
    return pl.pallas_call(
        functools.partial(place_kernel, (len(own), len(partner)), capacity, home_count, clear),
        in_specs=[SMEM] + [VMEM] * len(sources) + [ANY if clear else HBM],
        out_specs=[HBM, SMEM],
        out_shape=[out_type, jax.ShapeDtypeStruct((1,), jnp.int32)],
        input_output_aliases={} if clear else {len(sources) + 1: 0},
        scratch_shapes=[
            pltpu.SMEM((len(sources), LABEL_ROWS, 1, LANES), F32),
            pltpu.VMEM((PACK, 8, 1, LANES), F32),
            pltpu.SemaphoreType.DMA((len(sources),)),
            pltpu.SemaphoreType.DMA,
            pltpu.SemaphoreType.DMA,
        ],
        compiler_params=pltpu.CompilerParams(vmem_limit_bytes=32 * 2**20),
        cost_estimate=SMALL,
    )(me, *sources, token if clear else out)


def gate_kernel(value_ref, token_ref, other_ref, out_ref):
    out_ref[...] = value_ref[...]


def gate(value, token, other):
    return pl.pallas_call(
        gate_kernel,
        in_specs=[VMEM, ANY, ANY],
        out_specs=VMEM,
        out_shape=jax.ShapeDtypeStruct(value.shape, value.dtype),
        compiler_params=pltpu.CompilerParams(vmem_limit_bytes=24 * 2**20),
        cost_estimate=SMALL,
    )(value, token, other)


def most_kernel(bounds_ref, token_ref, most_ref):
    most_ref[0] = jnp.max(bounds_ref[...]).astype(jnp.int32)


def body(blocks, prolong, columns, aggregate, column_slot, owner_row):
    fine_rows = blocks.shape[0]
    home_count = owner_row.shape[0]
    size_gx = lax.axis_size("gx")
    size_gy = lax.axis_size("gy")
    size = size_gx * size_gy
    axes = ("gx", "gy")
    here_gx = lax.axis_index("gx")
    here_gy = lax.axis_index("gy")
    position = lax.axis_index(axes)
    bucket_rows = home_count // size_gx + 1
    most = bucket_rows * ROW_BLOCKS
    capacity = bucket_rows * FIRST_ROUND // 2
    most_fine = -(-bucket_rows * MOST_FINE // GROUP) * GROUP
    me = jnp.stack([here_gx, position, here_gy % 2]).astype(jnp.int32)

    block_view = (
        blocks.reshape(fine_rows, NNZ, PACK, LANES).transpose(0, 2, 1, 3).reshape(fine_rows, NNZ * PACK, LANES)
    )
    q_view = (
        prolong.reshape(fine_rows // 8, 8, PACK, LANES).transpose(0, 2, 1, 3).reshape(fine_rows * PACK, LANES)
    )
    edge_rows = 8 * PACK + 2 * NNZ * PACK + LABEL_ROWS
    backward = [(i, (i - 1) % size) for i in range(size)]
    forward = [(i, (i + 1) % size) for i in range(size)]
    back, forth = pl.pallas_call(
        edge_kernel,
        in_specs=[SMEM] * 3 + [ANY] * 2,
        out_specs=[VMEM] * 2,
        out_shape=[
            jax.ShapeDtypeStruct((edge_rows, LANES), F32),
            jax.ShapeDtypeStruct((8 * PACK, LANES), F32),
        ],
        scratch_shapes=[pltpu.SemaphoreType.DMA((4,))],
        compiler_params=pltpu.CompilerParams(vmem_limit_bytes=48 * 2**20),
        cost_estimate=SMALL,
    )(columns.T, column_slot.T, aggregate, q_view, block_view)
    edge = lax.ppermute(back, axes, backward)
    before = lax.ppermute(forth, axes, forward)

    factor_type = jax.ShapeDtypeStruct((fine_rows + BEFORE + AFTER, BS, LANES), BF16)
    right, bound = pl.pallas_call(
        functools.partial(prepare_kernel, fine_rows, home_count * size_gy, size_gx),
        in_specs=[SMEM] * 3 + [VMEM],
        out_specs=[VMEM] * 2,
        out_shape=[factor_type, jax.ShapeDtypeStruct((8, LANES), F32)],
        scratch_shapes=[pltpu.VMEM((8, BS, LANES), F32)],
        compiler_params=pltpu.CompilerParams(vmem_limit_bytes=32 * 2**20),
        cost_estimate=cost_of(5e-6),
    )(column_slot.T, aggregate, owner_row, q_view)
    right = pl.pallas_call(
        functools.partial(prepare_edge_kernel, fine_rows),
        in_specs=[VMEM] * 2 + [ANY],
        out_specs=ANY,
        out_shape=factor_type,
        input_output_aliases={2: 0},
        scratch_shapes=[
            pltpu.VMEM((AFTER + BEFORE, BS, LANES), BF16),
            pltpu.VMEM((AFTER + BEFORE, BS, LANES), F32),
            pltpu.SemaphoreType.DMA((2,)),
        ],
        compiler_params=pltpu.CompilerParams(vmem_limit_bytes=32 * 2**20),
        cost_estimate=SMALL,
    )(before, edge, right)

    def bucket(shift, base, token, other):
        return pl.pallas_call(
            functools.partial(
                bucket_kernel,
                shift,
                base,
                capacity,
                fine_rows,
                fine_rows * size,
                home_count,
                home_count * size_gy,
            ),
            in_specs=[SMEM] * 5 + [ANY] * 2 + [VMEM] * 3 + [ANY] * 2,
            out_specs=VMEM,
            out_shape=jax.ShapeDtypeStruct((capacity * PACK + LABEL_ROWS, LANES), F32),
            scratch_shapes=[
                pltpu.VMEM((most_fine * 2 * BS, LANES), F32),
                pltpu.VMEM((GROUP, BS, LANES), F32),
                pltpu.SMEM((LABEL_ROWS, 1, LANES), F32),
                pltpu.SMEM((4 * NNZ + 2,), jnp.int32),
                pltpu.SMEM((most_fine + GROUP,), jnp.int32),
                pltpu.SMEM((most_fine + GROUP,), jnp.int32),
                pltpu.SMEM((most_fine + GROUP,), jnp.int32),
                pltpu.SMEM((bucket_rows * 8,), jnp.int32),
                pltpu.SemaphoreType.DMA,
                pltpu.SemaphoreType.DMA,
            ],
            compiler_params=pltpu.CompilerParams(vmem_limit_bytes=40 * 2**20),
            cost_estimate=SMALL,
        )(
            me,
            columns.T,
            column_slot.T,
            aggregate,
            owner_row,
            block_view,
            edge.reshape(-1, 1, LANES),
            edge,
            q_view,
            right,
            token,
            other,
        )

    def across(value, shift):
        pairs = [(source, source ^ shift) for source in range(size_gx)]
        return lax.ppermute(value, "gx", pairs)

    def partner(value):
        pairs = [(source, source ^ 1) for source in range(size_gy)]
        return lax.ppermute(value, "gy", pairs)

    def across_partner(value, shift):
        pairs = [
            (gx * size_gy + gy, (gx ^ shift) * size_gy + (gy ^ 1)) for gx in range(size_gx) for gy in range(size_gy)
        ]
        return lax.ppermute(value, axes, pairs)

    bits = [1 << bit for bit in range(size.bit_length() - 1)]

    def agreed_with(value, step):
        pairs = [(source, source ^ step) for source in range(size)]
        return jnp.maximum(value, lax.ppermute(value, axes, pairs))

    out_type = pltpu.HBM((SLOTS, 2 * home_count // 8, PACK, 8, 1, LANES), F32)

    def round_of(out, base):
        first = out is None
        own_sent = bucket(0, base, me, me)
        from_partner = {0: partner(own_sent)}
        sent = {0: own_sent}
        token = own_sent
        for shift in [2, 1] + list(range(3, size_gx)):
            sent[shift] = bucket(shift, base, token, me)
            if first and shift == 1:
                sent[1] = gate(sent[1], from_partner[0], me)
            token = sent[shift]
        from_partner[1] = across_partner(sent[1], 1)
        arrived = {shift: across(sent[shift], shift) for shift in range(1, size_gx)}
        place = functools.partial(
            placed_into, out_type=out_type, me=me, capacity=capacity, home_count=home_count, token=token
        )
        out, placed = place(out, own=[own_sent], partner=[from_partner[0]])
        for shift in range(2, size_gx):
            value = arrived[shift]
            if first and shift == 2:
                agreed = bound
                for step in [bit for bit in bits if 1 < bit < 2 * size_gy] + [1]:
                    agreed = agreed_with(agreed, step)
                value = gate(value, from_partner[1], agreed)
            if first and shift == 3:
                for step in [bit for bit in bits if bit >= 2 * size_gy]:
                    agreed = agreed_with(agreed, step)
                value = gate(value, placed, agreed)
            from_partner[shift] = partner(value)
        out, _ = place(out, own=[arrived[1]], partner=[from_partner[1]])
        out, _ = place(out, own=[arrived[2]], partner=[])
        for shift in range(3, size_gx):
            out, placed = place(out, own=[arrived[shift]], partner=[from_partner[shift - 1]])
        out, _ = place(out, own=[], partner=[from_partner[size_gx - 1]])
        return (out, agreed, placed) if first else out

    out, agreed, token = round_of(None, 0)
    most_used = pl.pallas_call(
        most_kernel,
        in_specs=[VMEM, SMEM],
        out_specs=SMEM,
        out_shape=jax.ShapeDtypeStruct((1,), jnp.int32),
        cost_estimate=SMALL,
    )(agreed, token)[0]
    for later in range(capacity, most, capacity):
        out = lax.cond(most_used > later, lambda out: round_of(out, later), lambda out: out, out)
    return (
        out.reshape(SLOTS, 2 * home_count // 8, PACK, 8, LANES)
        .transpose(1, 3, 0, 2, 4)
        .reshape(2 * home_count, SLOTS, BS * BS)
    )


def solution(mesh):
    placed = (
        P(("gx", "gy"), None, None),
        P(("gx", "gy"), None),
        P(("gx", "gy"), None),
        P(("gx", "gy")),
        P(("gx", "gy"), None),
        P(("gx", "gy")),
    )
    return jax.shard_map(
        body, mesh=mesh, in_specs=placed, out_specs=P(("gx", "gy"), None, None), check_vma=False
    )
```
